32 devices in a mesh: node: 16 (over z, x, core), grp: 2 (over y).
Axes of the slice: x: 2, y: 2, z: 4, core: 2. Of those that a mesh axis runs over, the one named last changes fastest.
Arguments:
- samples: bfloat16 [16384, 2048], P(('node', 'grp')), may hold values from -6 to 6
- diag_block: bfloat16 [16384, 1024], P(('node', 'grp')), may hold values from -0.1875 to 0.1875
- test_matrix: bfloat16 [16384, 2048], P('node'), may hold values from -6 to 6
- coeffs: bfloat16 [16384, 256], P(('node', 'grp')), may hold values from -0.1875 to 0.1875
- cross: bfloat16 [4096, 256], P('node'), may hold values from -0.375 to 0.375
- skeleton: int32 [16, 256], P('node'), may hold values from 0 to 1023, as said below
- counts: int32 [16], P('node'), may hold values from 64 to 256, as said below
- parent_slot: int32 [16], P('node'), may hold values from 0 to 1, as said below
Outputs:
- generators: bfloat16 [4096, 2048], P(('node', 'grp'))
- parent_samples: float32 [8192, 2048], P(('node', 'grp'))
The draws below stay inside these ranges and needn't reach their ends.
Inputs may be any that keep to these rules, and one draw needn't show every extreme that they name: Each row holds 256 distinct rows of the node; the first counts of them are its skeleton, the rest are ignored. `counts`: some node has exactly 256. `parent_slot`: two siblings hold different values.
All inputs are finite; a program needn't handle non-finite values.
Results may differ from the reference program's by a relative error of at most 0.006.
Values may be sent and summed in bfloat16 or wider, within the bound.
No kernel may reach another device: no remote copies, remote signals or barrier semaphores. Data moves between devices by JAX's collectives and lax.ppermute only.
A program may use at most 64 MiB of HBM per device.

```python
import jax
import jax.numpy as jnp
from jax import lax

M = 1024
S = 2048
K = 256
SIB_BIT = 2
NODES = 16


def draw_skeleton(key, part):
    key = jax.random.fold_in(key, 11)
    node_keys = jax.random.split(key, NODES)
    orders = jax.vmap(lambda one_key: jax.random.permutation(one_key, M))(node_keys)
    return orders[:, :K].astype(jnp.int32)


def draw_counts(key, part):
    key = jax.random.fold_in(key, 12)
    first_key, second_key = jax.random.split(key)
    values = jax.random.randint(first_key, (NODES,), K // 4, K + 1)
    fullest = jax.random.randint(second_key, (), 0, NODES)
    return values.at[fullest].set(K).astype(jnp.int32)


def draw_parent_slot(key, part):
    key = jax.random.fold_in(key, 13)
    base_bits = jax.random.randint(key, (NODES,), 0, 2)
    node_ids = jnp.arange(NODES)
    own_bit = node_ids >> SIB_BIT & 1
    lower_node = node_ids - (own_bit << SIB_BIT)
    return (base_bits[lower_node] ^ own_bit).astype(jnp.int32)


def shard_levels(own_key, dims, cuts, low, high):
    loudness = 1.0
    for axis_at, blocks in cuts:
        heights = jax.random.uniform(jax.random.fold_in(jax.random.fold_in(own_key, 6), axis_at), (blocks,), jnp.float32, low / len(cuts), high / len(cuts))
        loudness = loudness * jnp.repeat(jnp.exp(heights), dims[axis_at] // blocks).reshape((-1,) + (1,) * (len(dims) - 1 - axis_at))
    return loudness


def scatter_about(rng, shape, scale, reach, pieces=(), kind=jnp.bfloat16):
    factor_of = shard_levels(rng, shape, pieces, -0.22, 0.18) if pieces else 1.0
    values = jax.random.normal(rng, shape, jnp.float32) * scale * factor_of
    return jnp.minimum(jnp.maximum(values, -reach), reach).astype(kind)


def setup_inputs(seed: int = 0) -> dict:
    key_of = jax.random.split(jax.random.key(seed), 9)
    return {
        "samples": scatter_about(key_of[0], (NODES * M, S), 1.0, 6.0, ((0, 32),)),
        "diag_block": scatter_about(key_of[1], (NODES * M, M), M ** -0.5, 0.1875, ((0, 32),)),
        "test_matrix": scatter_about(key_of[2], (NODES * M, S), 1.0, 6.0, ((0, 16),)),
        "coeffs": scatter_about(key_of[3], (NODES * M, K), M ** -0.5, 0.1875, ((0, 32),)),
        "cross": scatter_about(key_of[4], (NODES * K, K), K ** -0.5, 0.375, ((0, 16),)),
        "skeleton": draw_skeleton(jax.random.fold_in(key_of[8], 71), 0),
        "counts": draw_counts(jax.random.fold_in(key_of[8], 71), 0),
        "parent_slot": draw_parent_slot(jax.random.fold_in(key_of[8], 71), 0),
    }


def reference(samples, diag_block, test_matrix, coeffs, cross, skeleton, counts, parent_slot):
    half_rows = M // 2
    node_samples = samples.reshape(NODES, M, S)
    node_diag = diag_block.reshape(NODES, M, M)
    node_tests = test_matrix.reshape(NODES, M, S)
    node_coeffs = coeffs.reshape(NODES, M, K)

    def one_node(items):
        block_samples, block_diag, block_tests, block_coeffs, chosen, count_now = items
        offdiag = (block_samples.astype(jnp.float32) - jnp.dot(block_diag, block_tests, preferred_element_type=jnp.float32)).astype(jnp.bfloat16)
        skel = jnp.take(offdiag, chosen, axis=0).astype(jnp.float32)
        summed = jnp.zeros((K, S), jnp.float32)
        for which in range(2):
            tests_part = block_tests[which * half_rows:(which + 1) * half_rows]
            coeff_part = block_coeffs[which * half_rows:(which + 1) * half_rows]
            inside = (chosen >= which * half_rows) & (chosen < (which + 1) * half_rows)
            local_index = jnp.clip(chosen - which * half_rows, 0, half_rows - 1).astype(jnp.int32)
            picked = jnp.take(tests_part, local_index, axis=0).astype(jnp.float32)
            partial_value = lax.dot_general(coeff_part, tests_part, (((0,), (0,)), ((), ())), preferred_element_type=jnp.float32)
            partial_value = partial_value + jnp.where(inside[:, None], picked, jnp.float32(0.0))
            partial_value = lax.optimization_barrier(partial_value.astype(jnp.bfloat16)).astype(jnp.float32)
            summed = summed + partial_value
        live_slots = (jnp.arange(K) < count_now)[:, None]
        generator = jnp.where(live_slots, summed, jnp.float32(0.0)).astype(jnp.bfloat16)
        return skel, generator

    skel, generator = lax.map(one_node, (node_samples, node_diag, node_tests, node_coeffs, skeleton, counts))
    node_ids = jnp.arange(NODES)
    partner = node_ids ^ (1 << SIB_BIT)
    live_all = (jnp.arange(K)[None, :] < counts[:, None])[:, :, None]
    mixed = jnp.einsum("nkj,njs->nks", cross.reshape(NODES, K, K).astype(jnp.float32), generator[partner].astype(jnp.float32), precision=lax.Precision.HIGHEST)
    parent = jnp.where(live_all, skel - mixed, jnp.float32(0.0))
    first_slot = (parent_slot == 0)[:, None, None]
    first_half = jnp.where(first_slot, parent, parent[partner])
    second_half = jnp.where(first_slot, parent[partner], parent)
    blocks = jnp.stack([first_half, second_half], axis=1).reshape(NODES * 2 * K, S)
    return generator.reshape(NODES * K, S), blocks
```

```python
import functools

import jax
import jax.numpy as jnp
from jax import lax
from jax.experimental import pallas as pl
from jax.experimental.pallas import tpu as pltpu
from jax.sharding import PartitionSpec as P

SIB_BIT = 2
CHUNKS = 4
BLOCK = 256
F32, BF16 = jnp.float32, jnp.bfloat16

VMEM = pl.BlockSpec(memory_space=pltpu.VMEM)
SMEM = pl.BlockSpec(memory_space=pltpu.SMEM)
ANY = pl.BlockSpec(memory_space=pl.ANY)


def swap(block, axis, distance):
    count = lax.axis_size(axis)
    route = []
    for low in range(count):
        high = low | 1 << distance
        if high != low and high < count:
            route += [(low, high), (high, low)]
    return lax.ppermute(block, axis, route)


def call(body, outs, in_specs, out_specs, operands, scratch=(), flops=0, moved=0, alias=None):
    return pl.pallas_call(
        body,
        out_shape=outs,
        in_specs=in_specs,
        out_specs=out_specs,
        scratch_shapes=list(scratch),
        input_output_aliases=alias or {},
        compiler_params=pltpu.CompilerParams(vmem_limit_bytes=40 * 2**20),
        cost_estimate=pl.CostEstimate(flops=flops, bytes_accessed=moved, transcendentals=0),
    )(*operands)


def hot_rows(skel_ref, first, rows, live):
    slots = skel_ref.shape[1]
    down = jnp.broadcast_to(skel_ref[...], (128, slots)).T
    alive = lax.broadcasted_iota(jnp.int32, (slots, 128), 0) < live
    down = jnp.where(alive, down - first, -1)
    lane = lax.broadcasted_iota(jnp.int32, (slots, 128), 1)
    parts = [jnp.where(down == lane + at, 1.0, 0.0).astype(BF16) for at in range(0, rows, 128)]
    return jnp.concatenate(parts, axis=1)


def mm(a, b):
    return jnp.dot(a, b, preferred_element_type=F32)


def mmt(a, b):
    return lax.dot_general(a, b, (((0,), (0,)), ((), ())), preferred_element_type=F32)


def first_body(slot_ref, count_ref, skel_ref, cross_ref, coeffs_ref, diag_ref, samples_ref, tests_ref,
               message_ref, cross_out_ref, hot_ref, diag_rows_ref,
               diag_buf, samples_buf, tests_buf, sems):
    group = lax.axis_index("grp")
    half, cap = coeffs_ref.shape
    width = samples_buf.shape[1]
    owner = slot_ref[0] == group
    copies = [
        pltpu.make_async_copy(diag_ref, diag_buf, sems.at[0]),
        pltpu.make_async_copy(samples_ref.at[:, pl.ds(0, width)], samples_buf, sems.at[1]),
        pltpu.make_async_copy(tests_ref.at[:, pl.ds(0, width)], tests_buf, sems.at[2]),
    ]
    for copy in copies:
        copy.start()
    live = count_ref[0]
    alive = lax.broadcasted_iota(jnp.int32, (cap, cap), 0) < live
    cross_out_ref[...] = jnp.where(alive, cross_ref[...].astype(F32), 0.0).astype(BF16)
    hot = hot_rows(skel_ref, group * half, half, live)
    hot_ref[...] = hot
    copies[0].wait()
    diag_rows = (-mm(hot, diag_buf[...])).astype(BF16)
    diag_rows_ref[...] = diag_rows
    copies[1].wait()
    copies[2].wait()

    @pl.when(owner)
    def _():
        message_ref[...] = coeffs_ref[...]

    @pl.when(jnp.logical_not(owner))
    def _():
        for at in range(0, width, cap):
            part = mm(hot, samples_buf[:, at:at + cap]) + mm(diag_rows, tests_buf[:, at:at + cap])
            message_ref[pl.ds(at, cap), :] = part.astype(BF16)


def skel_body(hot_ref, diag_rows_ref, samples_ref, tests_ref, *rest):
    outs = rest[:CHUNKS]
    samples_buf, tests_buf, sems = rest[CHUNKS:]
    width = outs[0].shape[1]
    copies = []
    for i in range(CHUNKS):
        cut = pl.ds(i * width, width)
        pair = (pltpu.make_async_copy(samples_ref.at[:, cut], samples_buf.at[:, cut], sems.at[0, i]),
                pltpu.make_async_copy(tests_ref.at[:, cut], tests_buf.at[:, cut], sems.at[1, i]))
        for copy in pair:
            copy.start()
        copies.append(pair)
    for i in range(CHUNKS):
        for copy in copies[i]:
            copy.wait()
        for at in range(0, width, BLOCK):
            cut = slice(i * width + at, i * width + at + BLOCK)
            part = mm(hot_ref[...], samples_buf[:, cut]) + mm(diag_rows_ref[...], tests_buf[:, cut])
            outs[i][:, at:at + BLOCK] = part.astype(BF16)


def send_body(index, slot_ref, count_ref, skel_ref, coeffs_ref, other_ref, own_ref, got_ref, tests_ref, out_ref):
    group = lax.axis_index("grp")
    half, cap = coeffs_ref.shape
    width = out_ref.shape[1]
    owner = slot_ref[0] == group

    @pl.when(owner)
    def _():
        if index == 0:
            for at in range(0, width, cap):
                out_ref[:, at:at + cap] = own_ref[:, at:at + cap] + got_ref[at:at + cap, :]
        else:
            out_ref[...] = own_ref[...] + got_ref[...]

    @pl.when(jnp.logical_not(owner))
    def _():
        live = count_ref[0]
        hot = hot_rows(skel_ref, 0, 2 * half, live)
        alive = lax.broadcasted_iota(jnp.int32, (cap, BLOCK), 0) < live
        mine = pl.ds(pl.multiple_of(group * half, half), half)
        theirs = pl.ds(pl.multiple_of((1 - group) * half, half), half)
        for at in range(0, width, BLOCK):
            cut = slice(index * width + at, index * width + at + BLOCK)
            part = (mmt(coeffs_ref[...], tests_ref[mine, cut]) + mmt(other_ref[...], tests_ref[theirs, cut])
                    + mm(hot, tests_ref[:, cut]))
            out_ref[:, at:at + BLOCK] = jnp.where(alive, part, 0.0).astype(BF16)


def generator_body(count_ref, skel_ref, coeffs_ref, other_ref, tests_ref, out_ref):
    group = lax.axis_index("grp")
    half = coeffs_ref.shape[0]
    share, width = out_ref.shape
    live = count_ref[0]
    hot = hot_rows(skel_ref, 0, 2 * half, live)
    hot = jnp.where(group == 0, hot[:share].astype(F32), hot[share:].astype(F32)).astype(BF16)
    coeffs = jnp.where(group == 0, coeffs_ref[:, :share].astype(F32), coeffs_ref[:, share:].astype(F32)).astype(BF16)
    alive = lax.broadcasted_iota(jnp.int32, (share, BLOCK), 0) + group * share < live
    mine = pl.ds(pl.multiple_of(group * half, half), half)
    theirs = pl.ds(pl.multiple_of((1 - group) * half, half), half)
    for at in range(0, width, BLOCK):
        cut = slice(at, at + BLOCK)
        part = (mmt(coeffs, tests_ref[mine, cut]) + mmt(other_ref[...], tests_ref[theirs, cut])
                + mm(hot, tests_ref[:, cut]))
        out_ref[:, cut] = jnp.where(alive, part, 0.0).astype(BF16)


def parent_body(index, slot_ref, cross_ref, cross_got_ref, sent_ref, got_ref, *rest):
    out_ref, buf, sem = rest[-3:]
    group = lax.axis_index("grp")
    width = sent_ref.shape[1]
    owner = slot_ref[0] == group

    @pl.when(owner)
    def _():
        buf[...] = sent_ref[...].astype(F32) - mm(cross_ref[...], got_ref[...])

    @pl.when(jnp.logical_not(owner))
    def _():
        buf[...] = got_ref[...].astype(F32) - mm(cross_got_ref[...], sent_ref[...])

    copy = pltpu.make_async_copy(buf, out_ref.at[:, pl.ds(index * width, width)], sem)
    copy.start()
    copy.wait()


def local(samples, diag_block, test_matrix, coeffs, cross, skeleton, counts, parent_slot):
    half, cap = coeffs.shape
    rows, cols = test_matrix.shape
    share = cap // 2
    width = cols // CHUNKS
    group = lax.axis_index("grp")
    like = jax.ShapeDtypeStruct

    message, cross_live, hot, diag_rows = call(
        first_body,
        (like((half, cap), BF16), like((cap, cap), BF16), like((cap, half), BF16), like((cap, rows), BF16)),
        [SMEM, SMEM, VMEM, VMEM, VMEM, ANY, ANY, ANY],
        (VMEM,) * 4,
        (parent_slot, counts, skeleton, cross, coeffs, diag_block, samples, test_matrix),
        [pltpu.VMEM((half, rows), BF16), pltpu.VMEM((half, width), BF16), pltpu.VMEM((rows, width), BF16),
         pltpu.SemaphoreType.DMA((3,))],
        flops=2 * cap * rows * (half + width), moved=2 * (half * rows + (half + rows) * width),
    )
    got = [swap(message, "grp", 0)]
    cross_got = swap(cross_live, "node", SIB_BIT)
    own = call(
        skel_body,
        [like((cap, width), BF16)] * CHUNKS,
        [VMEM, VMEM, ANY, ANY],
        [VMEM] * CHUNKS,
        (hot, diag_rows, samples, test_matrix),
        [pltpu.VMEM((half, cols), BF16), pltpu.VMEM((rows, cols), BF16), pltpu.SemaphoreType.DMA((2, CHUNKS))],
        flops=2 * cap * (rows + half) * cols, moved=2 * (half + rows + cap) * cols,
    )
    got += [swap(own[i], "grp", 0) for i in range(1, CHUNKS)]
    other_share = swap(lax.dynamic_slice_in_dim(coeffs, (1 - group) * share, share, 1), "grp", 0)
    out = None
    for i in range(CHUNKS):
        sent = call(
            functools.partial(send_body, i),
            like((cap, width), BF16),
            [SMEM, SMEM, VMEM, VMEM, VMEM, VMEM, VMEM, VMEM],
            VMEM,
            (parent_slot, counts, skeleton, coeffs, got[0], own[i], got[i], test_matrix),
            flops=4 * cap * rows * width, moved=2 * (rows + 2 * cap) * width,
        )
        arrived = swap(sent, "node", SIB_BIT)
        out = call(
            functools.partial(parent_body, i),
            like((cap, cols), F32),
            [SMEM, VMEM, VMEM, VMEM, VMEM] + ([] if out is None else [ANY]),
            ANY,
            (parent_slot, cross_live, cross_got, sent, arrived) + (() if out is None else (out,)),
            [pltpu.VMEM((cap, width), F32), pltpu.SemaphoreType.DMA],
            flops=2 * cap * cap * width, moved=8 * cap * width,
            alias=None if out is None else {5: 0},
        )
    generators = call(
        generator_body,
        like((share, cols), BF16),
        [SMEM, VMEM, VMEM, VMEM, VMEM],
        VMEM,
        (counts, skeleton, coeffs, other_share, test_matrix),
        flops=4 * share * rows * cols, moved=2 * (rows + share) * cols,
    )
    return generators, out


def solution(mesh):
    return jax.shard_map(
        local,
        mesh=mesh,
        in_specs=(
            P(("node", "grp"), None),
            P(("node", "grp"), None),
            P("node", None),
            P(("node", "grp"), None),
            P("node", None),
            P("node", None),
            P("node"),
            P("node"),
        ),
        out_specs=(P(("node", "grp"), None), P(("node", "grp"), None)),
        check_vma=False,
    )
```

```python
import functools

import jax
import jax.numpy as jnp
from jax import lax
from jax.experimental import pallas as pl
from jax.experimental.pallas import tpu as pltpu
from jax.sharding import PartitionSpec as P

SIB_BIT = 2
CHUNKS = 4
BLOCK = 256
DEAD = 2.0**20
F32, BF16, I32 = jnp.float32, jnp.bfloat16, jnp.int32

VMEM = pl.BlockSpec(memory_space=pltpu.VMEM)
SMEM = pl.BlockSpec(memory_space=pltpu.SMEM)
HBM = pl.BlockSpec(memory_space=pltpu.HBM)
ANY = pl.BlockSpec(memory_space=pl.ANY)
like = jax.ShapeDtypeStruct


def swap(block, axis, distance):
    count = lax.axis_size(axis)
    route = []
    for low in range(count):
        high = low | 1 << distance
        if high != low and high < count:
            route += [(low, high), (high, low)]
    return lax.ppermute(block, axis, route)


def call(body, outs, in_specs, out_specs, operands, scratch=(), flops=0, moved=0, alias=None, limit=24):
    return pl.pallas_call(
        body,
        name=getattr(body, "func", body).__name__,
        out_shape=outs,
        in_specs=in_specs,
        out_specs=out_specs,
        scratch_shapes=list(scratch),
        input_output_aliases=alias or {},
        compiler_params=pltpu.CompilerParams(vmem_limit_bytes=limit * 2**20),
        cost_estimate=pl.CostEstimate(flops=flops, bytes_accessed=moved, transcendentals=0),
    )(*operands)


def mm(a, b):
    return jnp.dot(a, b, preferred_element_type=F32)


def hot_rows(skel, rows):
    slots = skel.shape[1]
    down = jnp.broadcast_to(skel, (128, slots)).T
    lane = lax.broadcasted_iota(I32, (slots, 128), 1)
    parts = [jnp.where(down == lane + at, 1.0, 0.0).astype(BF16) for at in range(0, rows, 128)]
    return jnp.concatenate(parts, axis=1)


def turned(coeffs):
    return coeffs.astype(F32).T.astype(BF16)


def is_owner(meta_ref):
    return jnp.max(meta_ref[0:1, :]) > 0


def alive_rows(meta_ref, shape, first=0):
    return lax.broadcasted_iota(I32, shape, 0) + first < jnp.max(meta_ref[1:2, :])


def own_half(group, half):
    return pl.ds(pl.multiple_of(group * half, half), half)


def first_body(slot_ref, skel_ref, coeffs_ref, cross_ref, diag_ref, samples_ref, tests_ref,
               message_ref, hot_ref, diag_rows_ref, meta_ref, cross_out_ref,
               skel_buf, coeffs_buf, diag_buf, samples_buf, tests_buf, sems):
    group = lax.axis_index("grp")
    half = coeffs_ref.shape[0]
    width = samples_buf.shape[1]
    pairs = [(skel_ref, skel_buf), (diag_ref, diag_buf), (samples_ref.at[:, pl.ds(0, width)], samples_buf),
             (tests_ref.at[:, pl.ds(0, width)], tests_buf), (coeffs_ref, coeffs_buf), (cross_ref, cross_out_ref)]
    copies = [pltpu.make_async_copy(src, dst, sems.at[i]) for i, (src, dst) in enumerate(pairs)]
    for copy in copies:
        copy.start()
    owner = slot_ref[0] == group
    meta_ref[...] = jnp.zeros(meta_ref.shape, I32) + jnp.where(owner, 1, 0)
    copies[0].wait()
    hot = hot_rows(skel_buf[...], 2 * half)
    hot_ref[...] = hot
    copies[1].wait()
    mine = hot_ref[:, own_half(group, half)]
    diag_rows = (-mm(mine, diag_buf[...])).astype(BF16)
    diag_rows_ref[...] = diag_rows
    for copy in copies[2:]:
        copy.wait()

    @pl.when(owner)
    def _():
        message_ref[...] = turned(coeffs_buf[...])

    @pl.when(jnp.logical_not(owner))
    def _():
        for at in range(0, width, BLOCK):
            cut = slice(at, at + BLOCK)
            message_ref[:, cut] = (mm(mine, samples_buf[:, cut]) + mm(diag_rows, tests_buf[:, cut])).astype(BF16)


def skel_rows(group, out_ref, first, hot_ref, diag_rows_ref, samples_ref, tests_ref):
    half = samples_ref.shape[0]
    mine = hot_ref[:, own_half(group, half)]
    for at in range(0, out_ref.shape[1], BLOCK):
        cut = slice(first + at, first + at + BLOCK)
        out_ref[:, at:at + BLOCK] = (
            mm(mine, samples_ref[:, cut]) + mm(diag_rows_ref[...], tests_ref[:, cut])).astype(BF16)


def next_body(owner_ref, count_ref, coeffs_ref, hot_ref, diag_rows_ref, samples_ref, tests_ref,
              own_ref, second_ref, partial_ref, slots_ref, meta_ref, coeffs_buf, sem):
    group = lax.axis_index("grp")
    half = coeffs_ref.shape[0]
    width = own_ref.shape[1]
    copy = pltpu.make_async_copy(coeffs_ref, coeffs_buf, sem)
    copy.start()
    owner = is_owner(owner_ref)
    meta_ref[0:1, :] = owner_ref[0:1, :]
    meta_ref[1:2, :] = jnp.zeros((1, 128), I32) + count_ref[0]
    skel_rows(group, second_ref, width, hot_ref, diag_rows_ref, samples_ref, tests_ref)
    copy.wait()

    @pl.when(owner)
    def _():
        skel_rows(group, own_ref, 0, hot_ref, diag_rows_ref, samples_ref, tests_ref)

    @pl.when(jnp.logical_not(owner))
    def _():
        slots = turned(coeffs_buf[...])
        slots_ref[...] = slots
        for at in range(0, width, BLOCK):
            cut = slice(at, at + BLOCK)
            partial_ref[:, cut] = mm(slots, tests_ref[own_half(group, half), cut]) + mm(hot_ref[...], tests_ref[:, cut])


def rest_body(meta_ref, slots_ref, hot_ref, diag_rows_ref, samples_ref, tests_ref, *outs):
    group = lax.axis_index("grp")
    others_ref = outs[-1]
    share = others_ref.shape[0]
    for i, out_ref in enumerate(outs[:-1]):
        skel_rows(group, out_ref, (i + 2) * out_ref.shape[1], hot_ref, diag_rows_ref, samples_ref, tests_ref)

    @pl.when(is_owner(meta_ref))
    def _():
        others_ref[...] = jnp.zeros(others_ref.shape, BF16)

    @pl.when(jnp.logical_not(is_owner(meta_ref)))
    def _():
        others_ref[...] = slots_ref[own_half(1 - group, share), :]


def send_body(index, meta_ref, first_got_ref, own_ref, got_ref, partial_ref, slots_ref, hot_ref, tests_ref, *rest):
    out_ref = rest[-1]
    group = lax.axis_index("grp")
    cap, width = out_ref.shape
    half = tests_ref.shape[0] // 2
    owner = is_owner(meta_ref)
    alive = alive_rows(meta_ref, (cap, BLOCK))

    @pl.when(owner)
    def _():
        for at in range(0, width, BLOCK):
            cut = slice(at, at + BLOCK)
            out_ref[:, cut] = jnp.where(alive, own_ref[:, cut].astype(F32) + got_ref[:, cut].astype(F32), DEAD).astype(BF16)

    @pl.when(jnp.logical_not(owner))
    def _():
        for at in range(0, width, BLOCK):
            cut = slice(index * width + at, index * width + at + BLOCK)
            part = mm(first_got_ref[...], tests_ref[own_half(1 - group, half), cut])
            if index == 0:
                part += partial_ref[:, cut]
            else:
                part += mm(slots_ref[...], tests_ref[own_half(group, half), cut]) + mm(hot_ref[...], tests_ref[:, cut])
            out_ref[:, at:at + BLOCK] = jnp.where(alive, part, 0.0).astype(BF16)


def generator_body(meta_ref, hot_ref, message_ref, others_ref, tests_ref, *rest):
    sent = rest[:CHUNKS]
    out_ref, token_ref, buf, sem = rest[CHUNKS + 1:]
    token_ref[...] = jnp.zeros(token_ref.shape, I32)
    group = lax.axis_index("grp")
    share, cols = out_ref.shape
    half = tests_ref.shape[0] // 2
    width = cols // CHUNKS
    owner = is_owner(meta_ref)
    rows = own_half(group, share)

    @pl.when(owner)
    def _():
        alive = alive_rows(meta_ref, (share, BLOCK), group * share)
        for at in range(0, cols, BLOCK):
            cut = slice(at, at + BLOCK)
            part = (mm(message_ref[rows, :], tests_ref[own_half(group, half), cut])
                    + mm(others_ref[...], tests_ref[own_half(1 - group, half), cut])
                    + mm(hot_ref[rows, :], tests_ref[:, cut]))
            buf[:, cut] = jnp.where(alive, part, 0.0).astype(BF16)

    @pl.when(jnp.logical_not(owner))
    def _():
        for i in range(CHUNKS):
            buf[:, i * width:(i + 1) * width] = sent[i][rows, :]

    copy = pltpu.make_async_copy(buf, out_ref, sem)
    copy.start()
    copy.wait()


def parent_body(index, token, meta_ref, cross_ref, cross_got_ref, sent_ref, got_ref, *rest):
    out_ref = rest[-3 - token]
    buf, sems = rest[-2:]
    if token:
        rest[-3][...] = jnp.zeros(rest[-3].shape, I32)
    width = sent_ref.shape[1]
    owner = is_owner(meta_ref)
    copies = [pltpu.make_async_copy(buf.at[:, pl.ds(at, BLOCK)], out_ref.at[:, pl.ds(index * width + at, BLOCK)],
                                    sems.at[at // BLOCK]) for at in range(0, width, BLOCK)]

    def work(skel_ref, rows_ref, gen_ref):
        for j, at in enumerate(range(0, width, BLOCK)):
            cut = pl.ds(at, BLOCK)
            skel = skel_ref[:, cut].astype(F32)
            buf[:, cut] = jnp.where(skel > DEAD / 2, 0.0, skel - mm(rows_ref[...], gen_ref[:, cut]))
            copies[j].start()

    @pl.when(owner)
    def _():
        work(sent_ref, cross_ref, got_ref)

    @pl.when(jnp.logical_not(owner))
    def _():
        work(got_ref, cross_got_ref, sent_ref)

    for copy in copies:
        copy.wait()


def local(samples, diag_block, test_matrix, coeffs, cross, skeleton, counts, parent_slot):
    half, cap = coeffs.shape
    rows, cols = test_matrix.shape
    share = cap // 2
    width = cols // CHUNKS
    dma = pltpu.SemaphoreType.DMA
    diag_far, coeffs_far, cross_far, skeleton_far, samples_far, tests_far = (
        pltpu.with_memory_space_constraint(x, pltpu.HBM)
        for x in (diag_block, coeffs, cross, skeleton, samples, test_matrix))
    piece = like((cap, width), BF16)

    message, hot, diag_rows, owner, cross_near = call(
        first_body,
        (piece, like((cap, rows), BF16), like((cap, rows), BF16), like((8, 128), I32), like((cap, cap), BF16)),
        [SMEM] + [HBM] * 6,
        (VMEM,) * 5,
        (parent_slot, skeleton_far, coeffs_far, cross_far, diag_far, samples_far, tests_far),
        [pltpu.VMEM((1, cap), I32), pltpu.VMEM((half, cap), BF16), pltpu.VMEM((half, rows), BF16),
         pltpu.VMEM((half, width), BF16), pltpu.VMEM((rows, width), BF16), dma((6,))],
        flops=2 * cap * rows * (half + width), moved=2 * (half * rows + (half + rows) * width),
    )
    got = [swap(message, "grp", 0)]
    cross_got = swap(cross_near, "node", SIB_BIT)
    own0, own1, partial, slots, meta = call(
        next_body,
        (piece, piece, like((cap, width), F32), like((cap, half), BF16), like((8, 128), I32)),
        [VMEM, SMEM, HBM] + [VMEM] * 4,
        (VMEM,) * 5,
        (owner, counts, coeffs_far, hot, diag_rows, samples, test_matrix),
        [pltpu.VMEM((half, cap), BF16), dma],
        flops=4 * cap * (rows + half) * width, moved=2 * (half + rows) * width,
    )
    got.append(swap(own1, "grp", 0))
    *own, others = call(
        rest_body,
        (piece,) * (CHUNKS - 2) + (like((share, half), BF16),),
        [VMEM] * 6,
        (VMEM,) * (CHUNKS - 1),
        (meta, slots, hot, diag_rows, samples, test_matrix),
        flops=2 * cap * (rows + half) * width * (CHUNKS - 2), moved=2 * half * width,
    )
    own = [own0, own1] + own
    got += [swap(x, "grp", 0) for x in own[2:]]
    others_got = swap(others, "grp", 0)
    out = None
    sents = []
    tokens = []
    for i in range(CHUNKS):
        hold = (tokens[i - 2],) if i >= 2 else (cross_got,) if i == 1 else ()
        sent = call(
            functools.partial(send_body, i),
            piece,
            [VMEM] * 8 + [ANY] * len(hold),
            VMEM,
            (meta, got[0], own[i], got[i], partial, slots, hot, test_matrix) + hold,
            flops=2 * cap * half * width * (1 if i == 0 else 4), moved=4 * cap * width,
        )
        sents.append(sent)
        arrived = swap(sent, "node", SIB_BIT)
        if i == CHUNKS - 1:
            generators, token = call(
                generator_body,
                (like((share, cols), BF16), like((8, 128), I32)),
                [VMEM] * (5 + CHUNKS) + [ANY],
                (HBM, VMEM),
                (meta, hot, message, others_got, test_matrix, *sents, tokens[-1]),
                [pltpu.VMEM((share, cols), BF16), dma],
                flops=4 * share * rows * cols, moved=2 * (rows + share) * cols,
            )
            tokens.append(token)
        token = i < CHUNKS - 1
        out, *more = call(
            functools.partial(parent_body, i, token),
            [like((cap, cols), F32)] + [like((8, 128), I32)] * token,
            [VMEM] * 5 + ([] if out is None else [HBM]) + [ANY] * (not token),
            [HBM] + [VMEM] * token,
            (meta, cross_near, cross_got, sent, arrived) + (() if out is None else (out,)) + tuple(tokens[-1:] * (not token)),
            [pltpu.VMEM((cap, width), F32), dma((width // BLOCK,))],
            flops=2 * cap * cap * width, moved=8 * cap * width,
            alias=None if out is None else {5: 0},
        )
        tokens += more
    return generators, out


def solution(mesh):
    return jax.shard_map(
        local,
        mesh=mesh,
        in_specs=(
            P(("node", "grp"), None),
            P(("node", "grp"), None),
            P("node", None),
            P(("node", "grp"), None),
            P("node", None),
            P("node", None),
            P("node"),
            P("node"),
        ),
        out_specs=(P(("node", "grp"), None), P(("node", "grp"), None)),
        check_vma=False,
    )
```

```python
import functools

import jax
import jax.numpy as jnp
from jax import lax
from jax.experimental import pallas as pl
from jax.experimental.pallas import tpu as pltpu
from jax.sharding import PartitionSpec as P

SIB_BIT = 2
CHUNKS = 4
BLOCK = 256
READY = 2
DEAD = 2.0**20
F32, BF16, I32 = jnp.float32, jnp.bfloat16, jnp.int32

VMEM = pl.BlockSpec(memory_space=pltpu.VMEM)
SMEM = pl.BlockSpec(memory_space=pltpu.SMEM)
HBM = pl.BlockSpec(memory_space=pltpu.HBM)
ANY = pl.BlockSpec(memory_space=pl.ANY)
like = jax.ShapeDtypeStruct


def swap(block, axis, distance):
    count = lax.axis_size(axis)
    route = []
    for low in range(count):
        high = low | 1 << distance
        if high != low and high < count:
            route += [(low, high), (high, low)]
    return lax.ppermute(block, axis, route)


def call(body, outs, in_specs, out_specs, operands, scratch=(), flops=0, moved=0, alias=None, limit=24):
    return pl.pallas_call(
        body,
        name=getattr(body, "func", body).__name__,
        out_shape=outs,
        in_specs=in_specs,
        out_specs=out_specs,
        scratch_shapes=list(scratch),
        input_output_aliases=alias or {},
        compiler_params=pltpu.CompilerParams(vmem_limit_bytes=limit * 2**20),
        cost_estimate=pl.CostEstimate(flops=flops, bytes_accessed=moved, transcendentals=0),
    )(*operands)


def mm(a, b):
    return jnp.dot(a, b, preferred_element_type=F32)


def hot_rows(skel, rows):
    slots = skel.shape[1]
    down = jnp.broadcast_to(skel, (128, slots)).T
    lane = lax.broadcasted_iota(I32, (slots, 128), 1)
    parts = [jnp.where(down == lane + at, 1.0, 0.0).astype(BF16) for at in range(0, rows, 128)]
    return jnp.concatenate(parts, axis=1)


def turned(coeffs):
    return coeffs.astype(F32).T.astype(BF16)


def is_owner(meta_ref):
    return jnp.max(meta_ref[0:1, :]) > 0


def alive_rows(meta_ref, shape, first=0):
    return lax.broadcasted_iota(I32, shape, 0) + first < jnp.max(meta_ref[1:2, :])


def own_half(group, half):
    return pl.ds(pl.multiple_of(group * half, half), half)


def first_body(slot_ref, skel_ref, coeffs_ref, cross_ref, diag_ref, samples_ref, tests_ref,
               message_ref, hot_ref, diag_rows_ref, meta_ref, cross_out_ref,
               skel_buf, coeffs_buf, diag_buf, samples_buf, tests_buf, sems):
    group = lax.axis_index("grp")
    half = coeffs_ref.shape[0]
    width = samples_buf.shape[1]
    pairs = [(skel_ref, skel_buf), (diag_ref, diag_buf), (samples_ref.at[:, pl.ds(0, width)], samples_buf),
             (tests_ref.at[:, pl.ds(0, width)], tests_buf), (coeffs_ref, coeffs_buf), (cross_ref, cross_out_ref)]
    copies = [pltpu.make_async_copy(src, dst, sems.at[i]) for i, (src, dst) in enumerate(pairs)]
    for copy in copies:
        copy.start()
    owner = slot_ref[0] == group
    meta_ref[...] = jnp.zeros(meta_ref.shape, I32) + jnp.where(owner, 1, 0)
    copies[0].wait()
    hot = hot_rows(skel_buf[...], 2 * half)
    hot_ref[...] = hot
    copies[1].wait()
    mine = hot_ref[:, own_half(group, half)]
    diag_rows = (-mm(mine, diag_buf[...])).astype(BF16)
    diag_rows_ref[...] = diag_rows
    for copy in copies[2:]:
        copy.wait()

    @pl.when(owner)
    def _():
        message_ref[...] = turned(coeffs_buf[...])

    @pl.when(jnp.logical_not(owner))
    def _():
        for at in range(0, width, BLOCK):
            cut = slice(at, at + BLOCK)
            message_ref[:, cut] = (mm(mine, samples_buf[:, cut]) + mm(diag_rows, tests_buf[:, cut])).astype(BF16)


def skel_rows(group, out_ref, first, hot_ref, diag_rows_ref, samples_ref, tests_ref):
    half = samples_ref.shape[0]
    mine = hot_ref[:, own_half(group, half)]
    for at in range(0, out_ref.shape[1], BLOCK):
        cut = slice(first + at, first + at + BLOCK)
        out_ref[:, at:at + BLOCK] = (
            mm(mine, samples_ref[:, cut]) + mm(diag_rows_ref[...], tests_ref[:, cut])).astype(BF16)


def next_body(owner_ref, count_ref, coeffs_ref, hot_ref, diag_rows_ref, samples_ref, tests_ref,
              own_ref, second_ref, partial_ref, slots_ref, meta_ref, coeffs_buf, sem):
    group = lax.axis_index("grp")
    half = coeffs_ref.shape[0]
    width = own_ref.shape[1]
    copy = pltpu.make_async_copy(coeffs_ref, coeffs_buf, sem)
    copy.start()
    owner = is_owner(owner_ref)
    meta_ref[0:1, :] = owner_ref[0:1, :]
    meta_ref[1:2, :] = jnp.zeros((1, 128), I32) + count_ref[0]
    skel_rows(group, second_ref, width, hot_ref, diag_rows_ref, samples_ref, tests_ref)
    copy.wait()

    @pl.when(owner)
    def _():
        skel_rows(group, own_ref, 0, hot_ref, diag_rows_ref, samples_ref, tests_ref)

    @pl.when(jnp.logical_not(owner))
    def _():
        slots = turned(coeffs_buf[...])
        slots_ref[...] = slots
        for at in range(0, width, BLOCK):
            cut = slice(at, at + BLOCK)
            partial_ref[:, cut] = mm(slots, tests_ref[own_half(group, half), cut]) + mm(hot_ref[...], tests_ref[:, cut])


def rest_body(meta_ref, slots_ref, hot_ref, diag_rows_ref, samples_ref, tests_ref, *outs):
    group = lax.axis_index("grp")
    others_ref = outs[-1]
    share = others_ref.shape[0]
    for i, out_ref in enumerate(outs[:-1]):
        skel_rows(group, out_ref, (i + 2) * out_ref.shape[1], hot_ref, diag_rows_ref, samples_ref, tests_ref)

    @pl.when(is_owner(meta_ref))
    def _():
        others_ref[...] = jnp.zeros(others_ref.shape, BF16)

    @pl.when(jnp.logical_not(is_owner(meta_ref)))
    def _():
        others_ref[...] = slots_ref[own_half(1 - group, share), :]


def send_body(index, meta_ref, first_got_ref, own_ref, got_ref, partial_ref, slots_ref, hot_ref, tests_ref, *rest):
    out_ref = rest[-1]
    group = lax.axis_index("grp")
    cap, width = out_ref.shape
    half = tests_ref.shape[0] // 2
    owner = is_owner(meta_ref)
    alive = alive_rows(meta_ref, (cap, BLOCK))

    @pl.when(owner)
    def _():
        for at in range(0, width, BLOCK):
            cut = slice(at, at + BLOCK)
            out_ref[:, cut] = jnp.where(alive, own_ref[:, cut].astype(F32) + got_ref[:, cut].astype(F32), DEAD).astype(BF16)

    @pl.when(jnp.logical_not(owner))
    def _():
        for at in range(0, width, BLOCK):
            cut = slice(index * width + at, index * width + at + BLOCK)
            part = mm(first_got_ref[...], tests_ref[own_half(1 - group, half), cut])
            if index == 0:
                part += partial_ref[:, cut]
            elif index >= CHUNKS - READY:
                place = index * width + at - (CHUNKS - READY) * width
                part += partial_ref[:, place:place + BLOCK]
            else:
                part += mm(slots_ref[...], tests_ref[own_half(group, half), cut]) + mm(hot_ref[...], tests_ref[:, cut])
            out_ref[:, at:at + BLOCK] = jnp.where(alive, part, 0.0).astype(BF16)


def early_body(meta_ref, hot_ref, message_ref, slots_ref, tests_ref, share_ref, partial_ref):
    group = lax.axis_index("grp")
    share, cols = share_ref.shape
    half = tests_ref.shape[0] // 2
    first = cols - partial_ref.shape[1]
    owner = is_owner(meta_ref)
    rows = own_half(group, share)

    @pl.when(owner)
    def _():
        for at in range(0, cols, BLOCK):
            cut = slice(at, at + BLOCK)
            share_ref[:, cut] = (mm(message_ref[rows, :], tests_ref[own_half(group, half), cut])
                                 + mm(hot_ref[rows, :], tests_ref[:, cut]))

    @pl.when(jnp.logical_not(owner))
    def _():
        for at in range(first, cols, BLOCK):
            cut = slice(at, at + BLOCK)
            partial_ref[:, at - first:at - first + BLOCK] = (
                mm(slots_ref[...], tests_ref[own_half(group, half), cut]) + mm(hot_ref[...], tests_ref[:, cut]))


def generator_body(meta_ref, share_ref, others_ref, tests_ref, *rest):
    sent = rest[:CHUNKS]
    out_ref, token_ref, buf, sems = rest[CHUNKS + 1:]
    token_ref[...] = jnp.zeros(token_ref.shape, I32)
    group = lax.axis_index("grp")
    share, cols = out_ref.shape
    half = tests_ref.shape[0] // 2
    width = cols // CHUNKS
    owner = is_owner(meta_ref)
    rows = own_half(group, share)
    copies = [pltpu.make_async_copy(buf.at[:, pl.ds(i * width, width)], out_ref.at[:, pl.ds(i * width, width)], sems.at[i])
              for i in range(CHUNKS)]

    @pl.when(owner)
    def _():
        alive = alive_rows(meta_ref, (share, BLOCK), group * share)
        for i in range(CHUNKS):
            for at in range(i * width, (i + 1) * width, BLOCK):
                cut = slice(at, at + BLOCK)
                part = share_ref[:, cut] + mm(others_ref[...], tests_ref[own_half(1 - group, half), cut])
                buf[:, cut] = jnp.where(alive, part, 0.0).astype(BF16)
            copies[i].start()

    @pl.when(jnp.logical_not(owner))
    def _():
        for i in range(CHUNKS):
            buf[:, i * width:(i + 1) * width] = sent[i][rows, :]
            copies[i].start()

    for copy in copies:
        copy.wait()


def parent_body(index, token, meta_ref, cross_ref, cross_got_ref, sent_ref, got_ref, *rest):
    out_ref = rest[-3 - token]
    buf, sems = rest[-2:]
    if token:
        rest[-3][...] = jnp.zeros(rest[-3].shape, I32)
    width = sent_ref.shape[1]
    owner = is_owner(meta_ref)
    copies = [pltpu.make_async_copy(buf.at[:, pl.ds(at, BLOCK)], out_ref.at[:, pl.ds(index * width + at, BLOCK)],
                                    sems.at[at // BLOCK]) for at in range(0, width, BLOCK)]

    def work(skel_ref, rows_ref, gen_ref):
        for j, at in enumerate(range(0, width, BLOCK)):
            cut = pl.ds(at, BLOCK)
            skel = skel_ref[:, cut].astype(F32)
            buf[:, cut] = jnp.where(skel > DEAD / 2, 0.0, skel - mm(rows_ref[...], gen_ref[:, cut]))
            copies[j].start()

    @pl.when(owner)
    def _():
        work(sent_ref, cross_ref, got_ref)

    @pl.when(jnp.logical_not(owner))
    def _():
        work(got_ref, cross_got_ref, sent_ref)

    for copy in copies:
        copy.wait()


def local(samples, diag_block, test_matrix, coeffs, cross, skeleton, counts, parent_slot):
    half, cap = coeffs.shape
    rows, cols = test_matrix.shape
    share = cap // 2
    width = cols // CHUNKS
    dma = pltpu.SemaphoreType.DMA
    diag_far, coeffs_far, cross_far, skeleton_far, samples_far, tests_far = (
        pltpu.with_memory_space_constraint(x, pltpu.HBM)
        for x in (diag_block, coeffs, cross, skeleton, samples, test_matrix))
    piece = like((cap, width), BF16)

    message, hot, diag_rows, owner, cross_near = call(
        first_body,
        (piece, like((cap, rows), BF16), like((cap, rows), BF16), like((8, 128), I32), like((cap, cap), BF16)),
        [SMEM] + [HBM] * 6,
        (VMEM,) * 5,
        (parent_slot, skeleton_far, coeffs_far, cross_far, diag_far, samples_far, tests_far),
        [pltpu.VMEM((1, cap), I32), pltpu.VMEM((half, cap), BF16), pltpu.VMEM((half, rows), BF16),
         pltpu.VMEM((half, width), BF16), pltpu.VMEM((rows, width), BF16), dma((6,))],
        flops=2 * cap * rows * (half + width), moved=2 * (half * rows + (half + rows) * width),
    )
    got = [swap(message, "grp", 0)]
    cross_got = swap(cross_near, "node", SIB_BIT)
    own0, own1, partial, slots, meta = call(
        next_body,
        (piece, piece, like((cap, width), F32), like((cap, half), BF16), like((8, 128), I32)),
        [VMEM, SMEM, HBM] + [VMEM] * 4,
        (VMEM,) * 5,
        (owner, counts, coeffs_far, hot, diag_rows, samples, test_matrix),
        [pltpu.VMEM((half, cap), BF16), dma],
        flops=4 * cap * (rows + half) * width, moved=2 * (half + rows) * width,
    )
    got.append(swap(own1, "grp", 0))
    early, ready = call(
        early_body,
        (like((share, cols), F32), like((cap, READY * width), F32)),
        [VMEM] * 5,
        (VMEM, VMEM),
        (meta, hot, message, slots, test_matrix),
        flops=3 * share * rows * cols, moved=0,
    )
    *own, others = call(
        rest_body,
        (piece,) * (CHUNKS - 2) + (like((share, half), BF16),),
        [VMEM] * 6,
        (VMEM,) * (CHUNKS - 1),
        (meta, slots, hot, diag_rows, samples, test_matrix),
        flops=2 * cap * (rows + half) * width * (CHUNKS - 2), moved=2 * half * width,
    )
    own = [own0, own1] + own
    got += [swap(x, "grp", 0) for x in own[2:]]
    others_got = swap(others, "grp", 0)
    out = None
    sents = []
    tokens = []
    for i in range(CHUNKS):
        hold = (tokens[i - 2],) if i >= 2 else (cross_got,) if i == 1 else (ready,)
        sent = call(
            functools.partial(send_body, i),
            piece,
            [VMEM] * 8 + [ANY] * len(hold),
            VMEM,
            (meta, got[0], own[i], got[i], ready if i >= CHUNKS - READY else partial, slots, hot, test_matrix) + hold,
            flops=2 * cap * half * width * (1 if i == 0 else 4), moved=4 * cap * width,
        )
        sents.append(sent)
        arrived = swap(sent, "node", SIB_BIT)
        if i == CHUNKS - 1:
            generators, token = call(
                generator_body,
                (like((share, cols), BF16), like((8, 128), I32)),
                [VMEM] * (4 + CHUNKS) + [ANY],
                (HBM, VMEM),
                (meta, early, others_got, test_matrix, *sents, tokens[-1]),
                [pltpu.VMEM((share, cols), BF16), dma((CHUNKS,))],
                flops=4 * share * rows * cols, moved=2 * (rows + share) * cols,
            )
            tokens.append(token)
        token = i < CHUNKS - 1
        out, *more = call(
            functools.partial(parent_body, i, token),
            [like((cap, cols), F32)] + [like((8, 128), I32)] * token,
            [VMEM] * 5 + ([] if out is None else [HBM]) + [ANY] * (not token),
            [HBM] + [VMEM] * token,
            (meta, cross_near, cross_got, sent, arrived) + (() if out is None else (out,)) + tuple(tokens[-1:] * (not token)),
            [pltpu.VMEM((cap, width), F32), dma((width // BLOCK,))],
            flops=2 * cap * cap * width, moved=8 * cap * width,
            alias=None if out is None else {5: 0},
        )
        tokens += more
    return generators, out


def solution(mesh):
    return jax.shard_map(
        local,
        mesh=mesh,
        in_specs=(
            P(("node", "grp"), None),
            P(("node", "grp"), None),
            P("node", None),
            P(("node", "grp"), None),
            P("node", None),
            P("node", None),
            P("node"),
            P("node"),
        ),
        out_specs=(P(("node", "grp"), None), P(("node", "grp"), None)),
        check_vma=False,
    )
```

```python
import functools

import jax
import jax.numpy as jnp
from jax import lax
from jax.experimental import pallas as pl
from jax.experimental.pallas import tpu as pltpu
from jax.sharding import PartitionSpec as P

SIB_BIT = 2
CHUNKS = 4
BLOCK = 256
READY = 2
DEAD = 2.0**20
F32, BF16, I32 = jnp.float32, jnp.bfloat16, jnp.int32

VMEM = pl.BlockSpec(memory_space=pltpu.VMEM)
SMEM = pl.BlockSpec(memory_space=pltpu.SMEM)
HBM = pl.BlockSpec(memory_space=pltpu.HBM)
ANY = pl.BlockSpec(memory_space=pl.ANY)
like = jax.ShapeDtypeStruct


def swap(block, axis, distance):
    count = lax.axis_size(axis)
    route = []
    for low in range(count):
        high = low | 1 << distance
        if high != low and high < count:
            route += [(low, high), (high, low)]
    return lax.ppermute(block, axis, route)


def call(body, outs, in_specs, out_specs, operands, scratch=(), flops=0, moved=0, alias=None, limit=24):
    return pl.pallas_call(
        body,
        name=getattr(body, "func", body).__name__,
        out_shape=outs,
        in_specs=in_specs,
        out_specs=out_specs,
        scratch_shapes=list(scratch),
        input_output_aliases=alias or {},
        compiler_params=pltpu.CompilerParams(vmem_limit_bytes=limit * 2**20),
        cost_estimate=pl.CostEstimate(flops=flops, bytes_accessed=moved, transcendentals=0),
    )(*operands)


def mm(a, b):
    return jnp.dot(a, b, preferred_element_type=F32)


def hot_rows(skel, rows):
    slots = skel.shape[1]
    down = jnp.broadcast_to(skel, (128, slots)).T
    lane = lax.broadcasted_iota(I32, (slots, 128), 1)
    parts = [jnp.where(down == lane + at, 1.0, 0.0).astype(BF16) for at in range(0, rows, 128)]
    return jnp.concatenate(parts, axis=1)


def turned(coeffs):
    return coeffs.astype(F32).T.astype(BF16)


def is_owner(slot_ref):
    return slot_ref[0] == lax.axis_index("grp")


def alive_rows(count_ref, shape, first=0):
    return lax.broadcasted_iota(I32, shape, 0) + first < count_ref[0]


def own_half(group, half):
    return pl.ds(pl.multiple_of(group * half, half), half)


def first_body(slot_ref, skel_ref, coeffs_ref, cross_ref, diag_ref, samples_ref, tests_ref,
               message_ref, hot_ref, diag_rows_ref, cross_out_ref,
               skel_buf, coeffs_buf, diag_buf, samples_buf, tests_buf, sems):
    group = lax.axis_index("grp")
    half = coeffs_ref.shape[0]
    width = samples_buf.shape[1]
    pairs = [(skel_ref, skel_buf), (diag_ref, diag_buf), (samples_ref.at[:, pl.ds(0, width)], samples_buf),
             (tests_ref.at[:, pl.ds(0, width)], tests_buf), (coeffs_ref, coeffs_buf), (cross_ref, cross_out_ref)]
    copies = [pltpu.make_async_copy(src, dst, sems.at[i]) for i, (src, dst) in enumerate(pairs)]
    for copy in copies:
        copy.start()
    owner = is_owner(slot_ref)
    copies[0].wait()
    hot = hot_rows(skel_buf[...], 2 * half)
    hot_ref[...] = hot
    copies[1].wait()
    mine = hot_ref[:, own_half(group, half)]
    diag_rows = (-mm(mine, diag_buf[...])).astype(BF16)
    diag_rows_ref[...] = diag_rows
    for copy in copies[2:]:
        copy.wait()

    @pl.when(owner)
    def _():
        message_ref[...] = turned(coeffs_buf[...])

    @pl.when(jnp.logical_not(owner))
    def _():
        for at in range(0, width, BLOCK):
            cut = slice(at, at + BLOCK)
            message_ref[:, cut] = (mm(mine, samples_buf[:, cut]) + mm(diag_rows, tests_buf[:, cut])).astype(BF16)


def skel_rows(group, out_ref, first, hot_ref, diag_rows_ref, samples_ref, tests_ref):
    half = samples_ref.shape[0]
    mine = hot_ref[:, own_half(group, half)]
    for at in range(0, out_ref.shape[1], BLOCK):
        cut = slice(first + at, first + at + BLOCK)
        out_ref[:, at:at + BLOCK] = (
            mm(mine, samples_ref[:, cut]) + mm(diag_rows_ref[...], tests_ref[:, cut])).astype(BF16)


def next_body(slot_ref, count_ref, coeffs_ref, hot_ref, diag_rows_ref, samples_ref, tests_ref,
              own_ref, second_ref, partial_ref, slots_ref, coeffs_buf, sem):
    group = lax.axis_index("grp")
    half = coeffs_ref.shape[0]
    width = own_ref.shape[1]
    copy = pltpu.make_async_copy(coeffs_ref, coeffs_buf, sem)
    copy.start()
    owner = is_owner(slot_ref)
    skel_rows(group, second_ref, width, hot_ref, diag_rows_ref, samples_ref, tests_ref)
    copy.wait()

    @pl.when(owner)
    def _():
        skel_rows(group, own_ref, 0, hot_ref, diag_rows_ref, samples_ref, tests_ref)

    @pl.when(jnp.logical_not(owner))
    def _():
        slots = turned(coeffs_buf[...])
        slots_ref[...] = slots
        for at in range(0, width, BLOCK):
            cut = slice(at, at + BLOCK)
            partial_ref[:, cut] = mm(slots, tests_ref[own_half(group, half), cut]) + mm(hot_ref[...], tests_ref[:, cut])


def rest_body(slot_ref, slots_ref, hot_ref, diag_rows_ref, samples_ref, tests_ref, *outs):
    group = lax.axis_index("grp")
    others_ref = outs[-1]
    share = others_ref.shape[0]
    for i, out_ref in enumerate(outs[:-1]):
        skel_rows(group, out_ref, (i + 2) * out_ref.shape[1], hot_ref, diag_rows_ref, samples_ref, tests_ref)

    @pl.when(is_owner(slot_ref))
    def _():
        others_ref[...] = jnp.zeros(others_ref.shape, BF16)

    @pl.when(jnp.logical_not(is_owner(slot_ref)))
    def _():
        others_ref[...] = slots_ref[own_half(1 - group, share), :]


def send_body(index, slot_ref, count_ref, first_got_ref, own_ref, got_ref, partial_ref, slots_ref, hot_ref, tests_ref, *rest):
    out_ref = rest[-1]
    group = lax.axis_index("grp")
    cap, width = out_ref.shape
    half = tests_ref.shape[0] // 2
    owner = is_owner(slot_ref)
    alive = alive_rows(count_ref, (cap, BLOCK))

    @pl.when(owner)
    def _():
        for at in range(0, width, BLOCK):
            cut = slice(at, at + BLOCK)
            out_ref[:, cut] = jnp.where(alive, own_ref[:, cut].astype(F32) + got_ref[:, cut].astype(F32), DEAD).astype(BF16)

    @pl.when(jnp.logical_not(owner))
    def _():
        for at in range(0, width, BLOCK):
            cut = slice(index * width + at, index * width + at + BLOCK)
            part = mm(first_got_ref[...], tests_ref[own_half(1 - group, half), cut])
            if index == 0:
                part += partial_ref[:, cut]
            elif index >= CHUNKS - READY:
                place = index * width + at - (CHUNKS - READY) * width
                part += partial_ref[:, place:place + BLOCK]
            else:
                part += mm(slots_ref[...], tests_ref[own_half(group, half), cut]) + mm(hot_ref[...], tests_ref[:, cut])
            out_ref[:, at:at + BLOCK] = jnp.where(alive, part, 0.0).astype(BF16)


def early_body(slot_ref, hot_ref, message_ref, slots_ref, tests_ref, share_ref, partial_ref):
    group = lax.axis_index("grp")
    share, cols = share_ref.shape
    half = tests_ref.shape[0] // 2
    first = cols - partial_ref.shape[1]
    owner = is_owner(slot_ref)
    rows = own_half(group, share)

    @pl.when(owner)
    def _():
        for at in range(0, cols, BLOCK):
            cut = slice(at, at + BLOCK)
            share_ref[:, cut] = (mm(message_ref[rows, :], tests_ref[own_half(group, half), cut])
                                 + mm(hot_ref[rows, :], tests_ref[:, cut]))

    @pl.when(jnp.logical_not(owner))
    def _():
        for at in range(first, cols, BLOCK):
            cut = slice(at, at + BLOCK)
            partial_ref[:, at - first:at - first + BLOCK] = (
                mm(slots_ref[...], tests_ref[own_half(group, half), cut]) + mm(hot_ref[...], tests_ref[:, cut]))


def generator_body(slot_ref, count_ref, share_ref, others_ref, tests_ref, *rest):
    sent = rest[:CHUNKS]
    out_ref, token_ref, buf, sems = rest[CHUNKS + 1:]
    token_ref[...] = jnp.zeros(token_ref.shape, I32)
    group = lax.axis_index("grp")
    share, cols = out_ref.shape
    half = tests_ref.shape[0] // 2
    width = cols // CHUNKS
    owner = is_owner(slot_ref)
    rows = own_half(group, share)
    copies = [pltpu.make_async_copy(buf.at[:, pl.ds(i * width, width)], out_ref.at[:, pl.ds(i * width, width)], sems.at[i])
              for i in range(CHUNKS)]

    @pl.when(owner)
    def _():
        alive = alive_rows(count_ref, (share, BLOCK), group * share)
        for i in range(CHUNKS):
            for at in range(i * width, (i + 1) * width, BLOCK):
                cut = slice(at, at + BLOCK)
                part = share_ref[:, cut] + mm(others_ref[...], tests_ref[own_half(1 - group, half), cut])
                buf[:, cut] = jnp.where(alive, part, 0.0).astype(BF16)
            copies[i].start()

    @pl.when(jnp.logical_not(owner))
    def _():
        for i in range(CHUNKS):
            buf[:, i * width:(i + 1) * width] = sent[i][rows, :]
            copies[i].start()

    for copy in copies:
        copy.wait()


def parent_body(index, token, slot_ref, cross_ref, cross_got_ref, sent_ref, got_ref, *rest):
    out_ref = rest[-3 - token]
    buf, sems = rest[-2:]
    if token:
        rest[-3][...] = jnp.zeros(rest[-3].shape, I32)
    width = sent_ref.shape[1]
    owner = is_owner(slot_ref)
    copies = [pltpu.make_async_copy(buf.at[:, pl.ds(at, BLOCK)], out_ref.at[:, pl.ds(index * width + at, BLOCK)],
                                    sems.at[at // BLOCK]) for at in range(0, width, BLOCK)]

    def work(skel_ref, rows_ref, gen_ref):
        for j, at in enumerate(range(0, width, BLOCK)):
            cut = pl.ds(at, BLOCK)
            skel = skel_ref[:, cut].astype(F32)
            buf[:, cut] = jnp.where(skel > DEAD / 2, 0.0, skel - mm(rows_ref[...], gen_ref[:, cut]))
            copies[j].start()

    @pl.when(owner)
    def _():
        work(sent_ref, cross_ref, got_ref)

    @pl.when(jnp.logical_not(owner))
    def _():
        work(got_ref, cross_got_ref, sent_ref)

    for copy in copies:
        copy.wait()


def local(samples, diag_block, test_matrix, coeffs, cross, skeleton, counts, parent_slot):
    half, cap = coeffs.shape
    rows, cols = test_matrix.shape
    share = cap // 2
    width = cols // CHUNKS
    dma = pltpu.SemaphoreType.DMA
    diag_far, coeffs_far, cross_far, skeleton_far, samples_far, tests_far = (
        pltpu.with_memory_space_constraint(x, pltpu.HBM)
        for x in (diag_block, coeffs, cross, skeleton, samples, test_matrix))
    piece = like((cap, width), BF16)

    message, hot, diag_rows, cross_near = call(
        first_body,
        (piece, like((cap, rows), BF16), like((cap, rows), BF16), like((cap, cap), BF16)),
        [SMEM] + [HBM] * 6,
        (VMEM,) * 4,
        (parent_slot, skeleton_far, coeffs_far, cross_far, diag_far, samples_far, tests_far),
        [pltpu.VMEM((1, cap), I32), pltpu.VMEM((half, cap), BF16), pltpu.VMEM((half, rows), BF16),
         pltpu.VMEM((half, width), BF16), pltpu.VMEM((rows, width), BF16), dma((6,))],
        flops=2 * cap * rows * (half + width), moved=2 * (half * rows + (half + rows) * width),
    )
    got = [swap(message, "grp", 0)]
    cross_got = swap(cross_near, "node", SIB_BIT)
    own0, own1, partial, slots = call(
        next_body,
        (piece, piece, like((cap, width), F32), like((cap, half), BF16)),
        [SMEM, SMEM, HBM] + [VMEM] * 4,
        (VMEM,) * 4,
        (parent_slot, counts, coeffs_far, hot, diag_rows, samples, test_matrix),
        [pltpu.VMEM((half, cap), BF16), dma],
        flops=4 * cap * (rows + half) * width, moved=2 * (half + rows) * width,
    )
    got.append(swap(own1, "grp", 0))
    early, ready = call(
        early_body,
        (like((share, cols), F32), like((cap, READY * width), F32)),
        [SMEM] + [VMEM] * 4,
        (VMEM, VMEM),
        (parent_slot, hot, message, slots, test_matrix),
        flops=3 * share * rows * cols, moved=0,
    )
    *own, others = call(
        rest_body,
        (piece,) * (CHUNKS - 2) + (like((share, half), BF16),),
        [SMEM] + [VMEM] * 5,
        (VMEM,) * (CHUNKS - 1),
        (parent_slot, slots, hot, diag_rows, samples, test_matrix),
        flops=2 * cap * (rows + half) * width * (CHUNKS - 2), moved=2 * half * width,
    )
    own = [own0, own1] + own
    got += [swap(x, "grp", 0) for x in own[2:]]
    others_got = swap(others, "grp", 0)
    out = None
    sents = []
    tokens = []
    for i in range(CHUNKS):
        hold = (tokens[i - 2],) if i >= 2 else (cross_got,) if i == 1 else (ready, cross_got)
        sent = call(
            functools.partial(send_body, i),
            piece,
            [SMEM] * 2 + [VMEM] * 7 + [ANY] * len(hold),
            VMEM,
            (parent_slot, counts, got[0], own[i], got[i], ready if i >= CHUNKS - READY else partial, slots, hot, test_matrix) + hold,
            flops=2 * cap * half * width * (1 if i == 0 else 4), moved=4 * cap * width,
        )
        sents.append(sent)
        arrived = swap(sent, "node", SIB_BIT)
        if i == CHUNKS - 1:
            generators, token = call(
                generator_body,
                (like((share, cols), BF16), like((8, 128), I32)),
                [SMEM] * 2 + [VMEM] * (3 + CHUNKS) + [ANY],
                (HBM, VMEM),
                (parent_slot, counts, early, others_got, test_matrix, *sents, tokens[-1]),
                [pltpu.VMEM((share, cols), BF16), dma((CHUNKS,))],
                flops=32 * share * rows * cols, moved=16 * (rows + share) * cols,
            )
            tokens.append(token)
        token = i < CHUNKS - 1
        out, *more = call(
            functools.partial(parent_body, i, token),
            [like((cap, cols), F32)] + [like((8, 128), I32)] * token,
            [SMEM] + [VMEM] * 4 + ([] if out is None else [HBM]) + [ANY] * (not token),
            [HBM] + [VMEM] * token,
            (parent_slot, cross_near, cross_got, sent, arrived) + (() if out is None else (out,)) + tuple(tokens[-1:] * (not token)),
            [pltpu.VMEM((cap, width), F32), dma((width // BLOCK,))],
            flops=2 * cap * cap * width, moved=8 * cap * width,
            alias=None if out is None else {5: 0},
        )
        tokens += more
    return generators, out


def solution(mesh):
    return jax.shard_map(
        local,
        mesh=mesh,
        in_specs=(
            P(("node", "grp"), None),
            P(("node", "grp"), None),
            P("node", None),
            P(("node", "grp"), None),
            P("node", None),
            P("node", None),
            P("node"),
            P("node"),
        ),
        out_specs=(P(("node", "grp"), None), P(("node", "grp"), None)),
        check_vma=False,
    )
```

```python
import functools

import jax
import jax.numpy as jnp
from jax import lax
from jax.experimental import pallas as pl
from jax.experimental.pallas import tpu as pltpu
from jax.sharding import PartitionSpec as P

SIB_BIT = 2
CHUNKS = 4
BLOCK = 256
READY = 2
DEAD = 2.0**20
F32, BF16, I32 = jnp.float32, jnp.bfloat16, jnp.int32

VMEM = pl.BlockSpec(memory_space=pltpu.VMEM)
SMEM = pl.BlockSpec(memory_space=pltpu.SMEM)
HBM = pl.BlockSpec(memory_space=pltpu.HBM)
ANY = pl.BlockSpec(memory_space=pl.ANY)
like = jax.ShapeDtypeStruct


def swap(block, axis, distance):
    count = lax.axis_size(axis)
    route = []
    for low in range(count):
        high = low | 1 << distance
        if high != low and high < count:
            route += [(low, high), (high, low)]
    return lax.ppermute(block, axis, route)


def call(body, outs, in_specs, out_specs, operands, scratch=(), flops=0, moved=0, alias=None, limit=24):
    return pl.pallas_call(
        body,
        name=getattr(body, "func", body).__name__,
        out_shape=outs,
        in_specs=in_specs,
        out_specs=out_specs,
        scratch_shapes=list(scratch),
        input_output_aliases=alias or {},
        compiler_params=pltpu.CompilerParams(vmem_limit_bytes=limit * 2**20),
        cost_estimate=pl.CostEstimate(flops=flops, bytes_accessed=moved, transcendentals=0),
    )(*operands)


def mm(a, b):
    return jnp.dot(a, b, preferred_element_type=F32)


def hot_rows(skel, rows):
    slots = skel.shape[1]
    down = jnp.broadcast_to(skel, (128, slots)).T
    lane = lax.broadcasted_iota(I32, (slots, 128), 1)
    parts = [jnp.where(down == lane + at, 1.0, 0.0).astype(BF16) for at in range(0, rows, 128)]
    return jnp.concatenate(parts, axis=1)


def turned(coeffs):
    return coeffs.astype(F32).T.astype(BF16)


def is_owner(slot_ref):
    return slot_ref[0] == lax.axis_index("grp")


def alive_rows(count_ref, shape, first=0):
    return lax.broadcasted_iota(I32, shape, 0) + first < count_ref[0]


def own_half(group, half):
    return pl.ds(pl.multiple_of(group * half, half), half)


def first_body(slot_ref, skel_ref, coeffs_ref, cross_ref, diag_ref, samples_ref, tests_ref,
               message_ref, hot_ref, diag_rows_ref, cross_out_ref,
               skel_buf, coeffs_buf, diag_buf, samples_buf, tests_buf, sems):
    group = lax.axis_index("grp")
    half = coeffs_ref.shape[0]
    width = samples_buf.shape[1]
    pairs = [(skel_ref, skel_buf), (diag_ref, diag_buf), (samples_ref.at[:, pl.ds(0, width)], samples_buf),
             (tests_ref.at[:, pl.ds(0, width)], tests_buf), (coeffs_ref, coeffs_buf), (cross_ref, cross_out_ref)]
    copies = [pltpu.make_async_copy(src, dst, sems.at[i]) for i, (src, dst) in enumerate(pairs)]
    for copy in copies:
        copy.start()
    owner = is_owner(slot_ref)
    copies[0].wait()
    hot = hot_rows(skel_buf[...], 2 * half)
    hot_ref[...] = hot
    copies[1].wait()
    mine = hot_ref[:, own_half(group, half)]
    diag_rows = (-mm(mine, diag_buf[...])).astype(BF16)
    diag_rows_ref[...] = diag_rows
    for copy in copies[2:]:
        copy.wait()

    @pl.when(owner)
    def _():
        message_ref[...] = turned(coeffs_buf[...])

    @pl.when(jnp.logical_not(owner))
    def _():
        for at in range(0, width, BLOCK):
            cut = slice(at, at + BLOCK)
            message_ref[:, cut] = (mm(mine, samples_buf[:, cut]) + mm(diag_rows, tests_buf[:, cut])).astype(BF16)


def skel_rows(group, out_ref, first, hot_ref, diag_rows_ref, samples_ref, tests_ref):
    half = samples_ref.shape[0]
    mine = hot_ref[:, own_half(group, half)]
    for at in range(0, out_ref.shape[1], BLOCK):
        cut = slice(first + at, first + at + BLOCK)
        out_ref[:, at:at + BLOCK] = (
            mm(mine, samples_ref[:, cut]) + mm(diag_rows_ref[...], tests_ref[:, cut])).astype(BF16)


def next_body(slot_ref, count_ref, coeffs_ref, hot_ref, diag_rows_ref, samples_ref, tests_ref,
              own_ref, second_ref, partial_ref, slots_ref, coeffs_buf, sem):
    group = lax.axis_index("grp")
    half = coeffs_ref.shape[0]
    width = own_ref.shape[1]
    copy = pltpu.make_async_copy(coeffs_ref, coeffs_buf, sem)
    copy.start()
    owner = is_owner(slot_ref)
    skel_rows(group, second_ref, width, hot_ref, diag_rows_ref, samples_ref, tests_ref)
    copy.wait()

    @pl.when(owner)
    def _():
        skel_rows(group, own_ref, 0, hot_ref, diag_rows_ref, samples_ref, tests_ref)

    @pl.when(jnp.logical_not(owner))
    def _():
        slots = turned(coeffs_buf[...])
        slots_ref[...] = slots
        for at in range(0, width, BLOCK):
            cut = slice(at, at + BLOCK)
            partial_ref[:, cut] = mm(slots, tests_ref[own_half(group, half), cut]) + mm(hot_ref[...], tests_ref[:, cut])


def rest_body(slot_ref, count_ref, slots_ref, hot_ref, diag_rows_ref, samples_ref, tests_ref, ready_ref, first_got_ref, *rest):
    outs, others_ref, done_ref = rest[-CHUNKS:-2], rest[-2], rest[-1]
    group = lax.axis_index("grp")
    share = others_ref.shape[0]
    cap, width = done_ref.shape
    half = tests_ref.shape[0] // 2
    first = tests_ref.shape[1] - width
    for i, out_ref in enumerate(outs):
        skel_rows(group, out_ref, (i + 2) * out_ref.shape[1], hot_ref, diag_rows_ref, samples_ref, tests_ref)

    @pl.when(is_owner(slot_ref))
    def _():
        others_ref[...] = jnp.zeros(others_ref.shape, BF16)

    @pl.when(jnp.logical_not(is_owner(slot_ref)))
    def _():
        others_ref[...] = slots_ref[own_half(1 - group, share), :]
        alive = alive_rows(count_ref, (cap, BLOCK))
        for at in range(0, width, BLOCK):
            part = ready_ref[:, at:at + BLOCK] + mm(
                first_got_ref[...], tests_ref[own_half(1 - group, half), first + at:first + at + BLOCK])
            done_ref[:, at:at + BLOCK] = jnp.where(alive, part, 0.0).astype(BF16)


def send_body(index, slot_ref, count_ref, first_got_ref, own_ref, got_ref, partial_ref, slots_ref, hot_ref, tests_ref, *rest):
    out_ref = rest[-1]
    group = lax.axis_index("grp")
    cap, width = out_ref.shape
    half = tests_ref.shape[0] // 2
    owner = is_owner(slot_ref)
    alive = alive_rows(count_ref, (cap, BLOCK))

    @pl.when(owner)
    def _():
        for at in range(0, width, BLOCK):
            cut = slice(at, at + BLOCK)
            out_ref[:, cut] = jnp.where(alive, own_ref[:, cut].astype(F32) + got_ref[:, cut].astype(F32), DEAD).astype(BF16)

    if index >= CHUNKS - READY:
        @pl.when(jnp.logical_not(owner))
        def _():
            place = (index - CHUNKS + READY) * width
            out_ref[...] = partial_ref[:, place:place + width]

        return

    @pl.when(jnp.logical_not(owner))
    def _():
        for at in range(0, width, BLOCK):
            cut = slice(index * width + at, index * width + at + BLOCK)
            part = mm(first_got_ref[...], tests_ref[own_half(1 - group, half), cut])
            if index == 0:
                part += partial_ref[:, cut]
            else:
                part += mm(slots_ref[...], tests_ref[own_half(group, half), cut]) + mm(hot_ref[...], tests_ref[:, cut])
            out_ref[:, at:at + BLOCK] = jnp.where(alive, part, 0.0).astype(BF16)


def early_body(slot_ref, hot_ref, message_ref, slots_ref, tests_ref, share_ref, partial_ref):
    group = lax.axis_index("grp")
    share, cols = share_ref.shape
    half = tests_ref.shape[0] // 2
    first = cols - partial_ref.shape[1]
    owner = is_owner(slot_ref)
    rows = own_half(group, share)

    @pl.when(owner)
    def _():
        for at in range(0, cols, BLOCK):
            cut = slice(at, at + BLOCK)
            share_ref[:, cut] = (mm(message_ref[rows, :], tests_ref[own_half(group, half), cut])
                                 + mm(hot_ref[rows, :], tests_ref[:, cut]))

    @pl.when(jnp.logical_not(owner))
    def _():
        for at in range(first, cols, BLOCK):
            cut = slice(at, at + BLOCK)
            partial_ref[:, at - first:at - first + BLOCK] = (
                mm(slots_ref[...], tests_ref[own_half(group, half), cut]) + mm(hot_ref[...], tests_ref[:, cut]))


def generator_body(slot_ref, count_ref, share_ref, others_ref, tests_ref, *rest):
    sent = rest[:CHUNKS]
    out_ref, token_ref, buf, sems = rest[CHUNKS + 1:]
    token_ref[...] = jnp.zeros(token_ref.shape, I32)
    group = lax.axis_index("grp")
    share, cols = out_ref.shape
    half = tests_ref.shape[0] // 2
    width = cols // CHUNKS
    owner = is_owner(slot_ref)
    rows = own_half(group, share)
    copies = [pltpu.make_async_copy(buf.at[:, pl.ds(i * width, width)], out_ref.at[:, pl.ds(i * width, width)], sems.at[i])
              for i in range(CHUNKS)]

    @pl.when(owner)
    def _():
        alive = alive_rows(count_ref, (share, BLOCK), group * share)
        for i in range(CHUNKS):
            for at in range(i * width, (i + 1) * width, BLOCK):
                cut = slice(at, at + BLOCK)
                part = share_ref[:, cut] + mm(others_ref[...], tests_ref[own_half(1 - group, half), cut])
                buf[:, cut] = jnp.where(alive, part, 0.0).astype(BF16)
            copies[i].start()

    @pl.when(jnp.logical_not(owner))
    def _():
        for i in range(CHUNKS):
            buf[:, i * width:(i + 1) * width] = sent[i][rows, :]
            copies[i].start()

    for copy in copies:
        copy.wait()


def parent_body(index, token, slot_ref, cross_ref, cross_got_ref, sent_ref, got_ref, *rest):
    out_ref = rest[-3 - token]
    buf, sems = rest[-2:]
    if token:
        rest[-3][...] = jnp.zeros(rest[-3].shape, I32)
    width = sent_ref.shape[1]
    owner = is_owner(slot_ref)
    copies = [pltpu.make_async_copy(buf.at[:, pl.ds(at, BLOCK)], out_ref.at[:, pl.ds(index * width + at, BLOCK)],
                                    sems.at[at // BLOCK]) for at in range(0, width, BLOCK)]

    def work(skel_ref, rows_ref, gen_ref):
        for j, at in enumerate(range(0, width, BLOCK)):
            cut = pl.ds(at, BLOCK)
            skel = skel_ref[:, cut].astype(F32)
            buf[:, cut] = jnp.where(skel > DEAD / 2, 0.0, skel - mm(rows_ref[...], gen_ref[:, cut]))
            copies[j].start()

    @pl.when(owner)
    def _():
        work(sent_ref, cross_ref, got_ref)

    @pl.when(jnp.logical_not(owner))
    def _():
        work(got_ref, cross_got_ref, sent_ref)

    for copy in copies:
        copy.wait()


def local(samples, diag_block, test_matrix, coeffs, cross, skeleton, counts, parent_slot):
    half, cap = coeffs.shape
    rows, cols = test_matrix.shape
    share = cap // 2
    width = cols // CHUNKS
    dma = pltpu.SemaphoreType.DMA
    diag_far, coeffs_far, cross_far, skeleton_far, samples_far, tests_far = (
        pltpu.with_memory_space_constraint(x, pltpu.HBM)
        for x in (diag_block, coeffs, cross, skeleton, samples, test_matrix))
    piece = like((cap, width), BF16)

    message, hot, diag_rows, cross_near = call(
        first_body,
        (piece, like((cap, rows), BF16), like((cap, rows), BF16), like((cap, cap), BF16)),
        [SMEM] + [HBM] * 6,
        (VMEM,) * 4,
        (parent_slot, skeleton_far, coeffs_far, cross_far, diag_far, samples_far, tests_far),
        [pltpu.VMEM((1, cap), I32), pltpu.VMEM((half, cap), BF16), pltpu.VMEM((half, rows), BF16),
         pltpu.VMEM((half, width), BF16), pltpu.VMEM((rows, width), BF16), dma((6,))],
        flops=2 * cap * rows * (half + width), moved=2 * (half * rows + (half + rows) * width),
    )
    got = [swap(message, "grp", 0)]
    cross_got = swap(cross_near, "node", SIB_BIT)
    own0, own1, partial, slots = call(
        next_body,
        (piece, piece, like((cap, width), F32), like((cap, half), BF16)),
        [SMEM, SMEM, HBM] + [VMEM] * 4,
        (VMEM,) * 4,
        (parent_slot, counts, coeffs_far, hot, diag_rows, samples, test_matrix),
        [pltpu.VMEM((half, cap), BF16), dma],
        flops=4 * cap * (rows + half) * width, moved=2 * (half + rows) * width,
    )
    got.append(swap(own1, "grp", 0))
    early, ready = call(
        early_body,
        (like((share, cols), F32), like((cap, READY * width), F32)),
        [SMEM] + [VMEM] * 4,
        (VMEM, VMEM),
        (parent_slot, hot, message, slots, test_matrix),
        flops=3 * share * rows * cols, moved=0,
    )
    *own, others, done = call(
        rest_body,
        (piece,) * (CHUNKS - 2) + (like((share, half), BF16), like((cap, READY * width), BF16)),
        [SMEM] * 2 + [VMEM] * 7,
        (VMEM,) * CHUNKS,
        (parent_slot, counts, slots, hot, diag_rows, samples, test_matrix, ready, got[0]),
        flops=2 * cap * (rows + half) * width * (CHUNKS - 2), moved=2 * half * width,
    )
    own = [own0, own1] + own
    got += [swap(x, "grp", 0) for x in own[2:]]
    others_got = swap(others, "grp", 0)
    out = None
    sents = []
    tokens = []
    for i in range(CHUNKS):
        hold = (tokens[i - 2],) if i >= 2 else (cross_got,) if i == 1 else (ready, cross_got)
        sent = call(
            functools.partial(send_body, i),
            piece,
            [SMEM] * 2 + [VMEM] * 7 + [ANY] * len(hold),
            VMEM,
            (parent_slot, counts, got[0], own[i], got[i], done if i >= CHUNKS - READY else partial, slots, hot, test_matrix) + hold,
            flops=2 * cap * half * width * (1 if i == 0 else 4), moved=4 * cap * width,
        )
        sents.append(sent)
        arrived = swap(sent, "node", SIB_BIT)
        if i == CHUNKS - 1:
            generators, token = call(
                generator_body,
                (like((share, cols), BF16), like((8, 128), I32)),
                [SMEM] * 2 + [VMEM] * (3 + CHUNKS) + [ANY],
                (HBM, VMEM),
                (parent_slot, counts, early, others_got, test_matrix, *sents, tokens[-1]),
                [pltpu.VMEM((share, cols), BF16), dma((CHUNKS,))],
                flops=32 * share * rows * cols, moved=16 * (rows + share) * cols,
            )
            tokens.append(token)
        token = i < CHUNKS - 1
        out, *more = call(
            functools.partial(parent_body, i, token),
            [like((cap, cols), F32)] + [like((8, 128), I32)] * token,
            [SMEM] + [VMEM] * 4 + ([] if out is None else [HBM]) + [ANY] * (not token),
            [HBM] + [VMEM] * token,
            (parent_slot, cross_near, cross_got, sent, arrived) + (() if out is None else (out,)) + tuple(tokens[-1:] * (not token)),
            [pltpu.VMEM((cap, width), F32), dma((width // BLOCK,))],
            flops=2 * cap * cap * width, moved=8 * cap * width,
            alias=None if out is None else {5: 0},
        )
        tokens += more
    return generators, out


def solution(mesh):
    return jax.shard_map(
        local,
        mesh=mesh,
        in_specs=(
            P(("node", "grp"), None),
            P(("node", "grp"), None),
            P("node", None),
            P(("node", "grp"), None),
            P("node", None),
            P("node", None),
            P("node"),
            P("node"),
        ),
        out_specs=(P(("node", "grp"), None), P(("node", "grp"), None)),
        check_vma=False,
    )
```
